32 devices in a mesh: cohort: 8 (over z, y), feat: 4 (over x, core).
Axes of the slice: x: 2, y: 2, z: 4, core: 2. Of those that a mesh axis runs over, the one named last changes fastest.
Arguments:
- b_factors: float32 [32, 8192, 256], P('cohort', 'feat'), may hold values from -0.375 to 0.375
- a_factors: float32 [32, 256, 8192], P('cohort', None, 'feat'), may hold values from -0.0625 to 0.0625
- ranks: int32 [32], P('cohort'), may hold values from 8 to 256, as said below
- probes: float32 [8192, 256], P('feat'), may hold values from -6 to 6
Outputs:
- subspace: float32 [8192, 256], P('feat')
The draws below stay inside these ranges and needn't reach their ends.
Inputs may be any that keep to these rules, and one draw needn't show every extreme that they name: `ranks`: each client's rank is 8 times a power of two; some client has rank 256 and some client has rank 8.
All inputs are finite; a program needn't handle non-finite values.
Results may differ from the reference program's by a relative error of at most 0.00011.
Values sent between devices are 32-bit elements; how exact they have to be, the bound alone decides.
No kernel may reach another device: no remote copies, remote signals or barrier semaphores. Data moves between devices by JAX's collectives and lax.ppermute only.
A program may use at most 64 MiB of HBM per device.

```python
import math
import jax
import jax.numpy as jnp
from jax import lax

D = 8192
P_SIZE = 256
RMAX = 256
CLI_DEV = 4
ITERS = 2
NS_STEPS = 5
CLIENTS = 32


def draw_ranks(key, part):
    levels = (RMAX // 8).bit_length()
    top_level = levels - 1
    tier_key = jax.random.fold_in(key, 11)
    level_key = jax.random.fold_in(key, 23)
    top_key = jax.random.fold_in(key, 37)
    low_key = jax.random.fold_in(key, 41)
    tiers = jax.random.randint(tier_key, (CLIENTS // CLI_DEV,), max(top_level - 2, 0), top_level + 1)
    spread_tiers = jnp.repeat(tiers, CLI_DEV, total_repeat_length=CLIENTS)
    lowest = jnp.maximum(spread_tiers - 2, 0)
    powers = jax.random.randint(level_key, (CLIENTS,), lowest, spread_tiers + 1)
    ranks = jnp.left_shift(jnp.full((CLIENTS,), 8, jnp.int32), powers.astype(jnp.int32))
    chosen = jax.random.randint(top_key, (), 0, CLIENTS)
    offset = jax.random.randint(low_key, (), 1, CLIENTS)
    smallest = (chosen + offset) % CLIENTS
    ranks = ranks.at[chosen].set(RMAX)
    ranks = ranks.at[smallest].set(8)
    return ranks.astype(jnp.int32)


def block_levels(key, extent, split, least, high):
    factor_of = 1.0
    for axis_at, blocks in split:
        draws = jax.random.uniform(jax.random.fold_in(jax.random.fold_in(key, 6), axis_at), (blocks,), jnp.float32, least / len(split), high / len(split))
        factor_of = factor_of * jnp.repeat(jnp.exp(draws), extent[axis_at] // blocks).reshape((-1,) + (1,) * (len(extent) - 1 - axis_at))
    return factor_of


def gaussian(key, dims, spread, reach, pieces=(), held_as=jnp.bfloat16):
    values = spread * jax.random.normal(key, dims, jnp.float32)
    if pieces:
        values = values * block_levels(key, dims, pieces, -0.22, 0.18)
    return jnp.clip(values, -reach, reach).astype(held_as)


def setup_inputs(seed: int = 0) -> dict:
    key_of = jax.random.split(jax.random.key(seed), 5)
    return {
        "b_factors": gaussian(key_of[0], (CLIENTS, D, RMAX), RMAX ** -0.5, 0.375, ((0, 8), (1, 4)), jnp.float32),
        "a_factors": gaussian(key_of[1], (CLIENTS, RMAX, D), D ** -0.5, 0.0625, ((0, 8), (2, 4)), jnp.float32),
        "ranks": draw_ranks(jax.random.fold_in(key_of[4], 71), 0),
        "probes": gaussian(key_of[3], (D, P_SIZE), 1.0, 6.0, ((0, 4),), jnp.float32),
    }


def live_table(ranks):
    slots = jnp.arange(RMAX, dtype=jnp.int32)
    return (slots[None, :] < ranks[:, None]).astype(jnp.float32)

def probe_panel(b_factors, a_factors, live, basis):

    def add_client(total, item):
        left, right, mask_row = item
        coef = jnp.dot(right, basis, precision=lax.Precision.HIGHEST, preferred_element_type=jnp.float32) * mask_row[:, None]
        return (total + jnp.dot(left, coef, precision=lax.Precision.HIGHEST, preferred_element_type=jnp.float32), None)
    total, unused = lax.scan(add_client, jnp.zeros((D, P_SIZE), jnp.float32), (b_factors, a_factors, live))
    return total

def orthonormal(panel):
    gram = jnp.dot(panel.T, panel, precision=lax.Precision.HIGHEST, preferred_element_type=jnp.float32)
    scale = lax.rsqrt(jnp.trace(gram))
    iterate = panel * scale
    for turn in range(NS_STEPS):
        inner = jnp.dot(iterate.T, iterate, precision=lax.Precision.HIGHEST, preferred_element_type=jnp.float32)
        iterate = 1.5 * iterate - 0.5 * jnp.dot(iterate, inner, precision=lax.Precision.HIGHEST, preferred_element_type=jnp.float32)
    return iterate

def reference(b_factors, a_factors, ranks, probes):
    live = live_table(ranks)
    basis = probes
    for turn in range(ITERS):
        basis = orthonormal(probe_panel(b_factors, a_factors, live, basis))
    return math.sqrt(D) * basis
```

```python
import math

import jax
import jax.numpy as jnp
from jax import lax
from jax.sharding import PartitionSpec as P

ITERS = 2
NS_STEPS = 5
GROUPS = 2


def product(left, right):
    return jnp.dot(left, right, precision=lax.Precision.HIGH, preferred_element_type=jnp.float32)


def coef_terms(a_factors, basis):
    return jnp.einsum("crd,dp->crp", a_factors, basis, precision=lax.Precision.HIGH, preferred_element_type=jnp.float32)


def panel_terms(b_factors, coef):
    return jnp.einsum("cdr,crp->dp", b_factors, coef, precision=lax.Precision.HIGH, preferred_element_type=jnp.float32)


class Grid:
    def __init__(self, mesh):
        self.cohorts = mesh.shape["cohort"]
        self.feats = mesh.shape["feat"]
        self.places = self.cohorts // 2
        cohort = lax.axis_index("cohort")
        self.place, self.side = cohort // 2, cohort % 2
        self.half = lax.axis_index("feat") % 2

    def across(self, block):
        return lax.ppermute(block, "cohort", [(i, i ^ 1) for i in range(self.cohorts)])

    def along(self, block):
        return lax.ppermute(block, "cohort", [(i, (i + 2) % self.cohorts) for i in range(self.cohorts)])

    def feat_swap(self, block, bit):
        return lax.ppermute(block, "feat", [(i, i ^ bit) for i in range(self.feats)])

    def feat_sum(self, part):
        rows = part.shape[0] // 2
        mine = lax.dynamic_slice(part, (self.half * rows, 0), (rows, part.shape[1]))
        other = lax.dynamic_slice(part, ((1 - self.half) * rows, 0), (rows, part.shape[1]))
        total = mine + self.feat_swap(other, 1)
        bit = 2
        while bit < self.feats:
            total = total + self.feat_swap(total, bit)
            bit *= 2
        partner = self.feat_swap(total, 1)
        low = jnp.where(self.half == 0, total, partner)
        high = jnp.where(self.half == 0, partner, total)
        return jnp.concatenate([low, high], 0)

    def scatter_sum(self, part):
        rows = part.shape[0] // self.cohorts

        def block(place, side):
            index = lax.rem(place + self.places, self.places) * 2 + side
            return lax.dynamic_slice(part, (index * rows, 0), (rows, part.shape[1]))

        total = None
        for step in range(1, self.places + 1):
            fresh = self.across(block(self.place - step, 1 - self.side)) + block(self.place - step, self.side)
            total = fresh if total is None else fresh + self.along(total)
        return total

    def gather(self, block):
        rows, columns = block.shape
        whole = jnp.zeros((self.cohorts * rows, columns), block.dtype)
        for step in range(self.places):
            place = lax.rem(self.place - step + self.places, self.places)
            whole = lax.dynamic_update_slice(whole, block, ((place * 2 + self.side) * rows, 0))
            whole = lax.dynamic_update_slice(whole, self.across(block), ((place * 2 + 1 - self.side) * rows, 0))
            if step < self.places - 1:
                block = self.along(block)
        return whole


def newton(gram):
    size = gram.shape[0]
    eye = jnp.eye(size, dtype=jnp.float32)
    scale = lax.rsqrt(jnp.trace(gram))
    inner = gram * (scale * scale)
    mixing = eye * scale
    for turn in range(NS_STEPS):
        factor = 1.5 * eye - 0.5 * inner
        mixing = product(mixing, factor) if turn else factor * scale
        if turn < NS_STEPS - 1:
            inner = product(product(inner, factor), factor)
    return mixing


def solution(mesh):
    def on_device(b_factors, a_factors, ranks, probes):
        grid = Grid(mesh)
        clients, rows, slots = b_factors.shape
        features = rows * grid.feats
        columns = probes.shape[1] // GROUPS
        live = (jnp.arange(slots, dtype=jnp.int32)[None, :] < ranks[:, None]).astype(jnp.float32)
        live = live.reshape(clients * slots, 1)

        def apply(basis, normalize):
            part = coef_terms(a_factors, basis).reshape(clients * slots, -1)
            scale = jnp.ones((), jnp.float32)
            if normalize:
                squares = jnp.full((16, part.shape[1]), jnp.sum(basis * basis), jnp.float32)
                part = jnp.concatenate([part, squares], 0)
            total = grid.feat_sum(part)
            if normalize:
                square = total[clients * slots, 0]
                scale = jnp.where(square > 0, lax.rsqrt(square), 1.0)
            coef = (total[: clients * slots] * (live * scale)).reshape(clients, slots, -1)
            return grid.gather(grid.scatter_sum(panel_terms(b_factors, coef))), scale

        mixing = None
        panels = [probes[:, g * columns : (g + 1) * columns] for g in range(GROUPS)]
        for turn in range(ITERS):
            done = [apply(panel, turn > 0) for panel in panels]
            panels = [panel for panel, scale in done]
            scales = jnp.concatenate([jnp.full((columns, 1), 1.0 / scale) for panel, scale in done], 0)
            panel = jnp.concatenate(panels, 1)
            gram = grid.feat_sum(product(panel.T, panel))
            if mixing is None:
                mixing = newton(gram)
            else:
                mixing = scales * mixing
                mixing = product(mixing, newton(product(mixing.T, product(gram, mixing))))
        return product(panel, mixing * math.sqrt(features))

    in_specs = (P("cohort", "feat", None), P("cohort", None, "feat"), P("cohort"), P("feat", None))
    return jax.shard_map(on_device, mesh=mesh, in_specs=in_specs, out_specs=P("feat", None), check_vma=False)
```

```python
import functools
import math

import jax
import jax.numpy as jnp
from jax import lax
from jax.experimental import pallas as pl
from jax.experimental.pallas import tpu as pltpu
from jax.sharding import PartitionSpec as P

ITERS = 2
NS_STEPS = 5
GROUPS = 2
EXTRA = 8
ROW_BLOCKS = 8
WHOLE = pl.BlockSpec(memory_space=pltpu.VMEM)
F32 = jnp.float32
BF16 = jnp.bfloat16


def split(value):
    high = value.astype(BF16)
    return high, (value - high.astype(F32)).astype(BF16)


def dot(left, right):
    return jnp.dot(left, right, preferred_element_type=F32)


def product(left, right):
    left_high, left_low = split(left)
    right_high, right_low = split(right)
    return dot(left_high, right_high) + (dot(left_high, right_low) + dot(left_low, right_high))


def wide_product(left, pair, width):
    high, low = split(left)
    both = dot(high, pair)
    return both[:, :width] + (both[:, width:] + dot(low, pair[:, :width]))


def params(mib):
    return pltpu.CompilerParams(vmem_limit_bytes=mib * 2**20)


def cost(flops, moved):
    return pl.CostEstimate(flops=int(flops), bytes_accessed=int(moved), transcendentals=0)


def coef_kernel(blocks, groups, squares, where, half, a_ref, *refs):
    step = pl.program_id(0)
    inputs, outputs, (pair, sums) = refs[:blocks], refs[blocks:-2], refs[-2:]
    rows, columns = inputs[0].shape

    @pl.when(step == 0)
    def _():
        for k in range(blocks):
            value = inputs[k][...]
            high, low = split(value)
            at = pl.ds(pl.multiple_of(where[k] * rows, rows), rows)
            pair[at, :columns] = high
            pair[at, columns:] = low
            if squares:
                sums[pl.ds(where[k], 1), :] = jnp.sum(value * value, axis=0, keepdims=True)
        if squares:
            total = jnp.sum(sums[...], axis=0, keepdims=True)
            total = jnp.sum(total, axis=1, keepdims=True)
            for out in outputs:
                out[out.shape[0] - EXTRA :, :] = jnp.broadcast_to(total, (EXTRA, out.shape[1]))

    result = wide_product(a_ref[...], pair[...], columns)
    tall = result.shape[0]
    each = columns // groups
    steps = pl.num_programs(0) // 2
    at = pl.ds(pl.multiple_of(lax.rem(step, steps) * tall, tall), tall)

    @pl.when(step < steps)
    def _():
        for g in range(groups):
            outputs[2 * g][at, :] = result[:, g * each : (g + 1) * each]

    @pl.when(step >= steps)
    def _():
        for g in range(groups):
            outputs[2 * g + 1][at, :] = result[:, g * each : (g + 1) * each]


def coef_terms(a_rows, basis, where, half, groups, squares):
    total, depth = a_rows.shape
    tall = total // ROW_BLOCKS
    steps = ROW_BLOCKS // 2
    columns = basis[0].shape[1]
    out_rows = total // 2 + (EXTRA if squares else 0)
    kernel = functools.partial(coef_kernel, len(basis), groups, squares)

    def a_place(step, where, half):
        return (lax.rem(step + (1 - half[0]) * steps, ROW_BLOCKS), 0)

    whole = lambda array: pl.BlockSpec(array.shape, lambda step, where, half: (0, 0))
    outs = [jax.ShapeDtypeStruct((out_rows, columns // groups), F32)] * (2 * groups)
    return pl.pallas_call(
        kernel,
        grid_spec=pltpu.PrefetchScalarGridSpec(
            num_scalar_prefetch=2,
            grid=(ROW_BLOCKS,),
            in_specs=[pl.BlockSpec((tall, depth), a_place)] + [whole(b) for b in basis],
            out_specs=[whole(out) for out in outs],
            scratch_shapes=[
                pltpu.VMEM((depth, 2 * columns), BF16),
                pltpu.VMEM((max(len(basis), 8), columns), F32),
            ],
        ),
        out_shape=outs,
        compiler_params=params(32),
        cost_estimate=cost(8 * total * depth * columns, 4 * total * depth),
        name="coef",
    )(where, half, a_rows, *basis)


def panel_kernel(squares, where, half, ranks, b_ref, mine_ref, partner_ref, *refs):
    step = pl.program_id(0)
    pair = refs[-1]
    clients, slots, width = pair.shape
    columns = width // 2

    @pl.when(step == 0)
    def _():
        scale = jnp.ones((1, columns), F32)
        if squares:
            square = mine_ref[mine_ref.shape[0] - EXTRA : mine_ref.shape[0] - EXTRA + 1, :]
            scale = jnp.where(square > 0, lax.rsqrt(square), 1.0)
            refs[-2][...] = jnp.broadcast_to(scale, refs[-2].shape)
        first = half[0] == 0
        for c in range(clients):
            at = pl.ds((c % (clients // 2)) * slots, slots)
            mine, partner = mine_ref[at, :], partner_ref[at, :]
            value = jnp.where(first, mine, partner) if c < clients // 2 else jnp.where(first, partner, mine)
            slot = lax.broadcasted_iota(jnp.int32, value.shape, 0)
            value = jnp.where(slot < ranks[c], value * scale, 0.0)
            high, low = split(value)
            pair[c, :, :columns] = high
            pair[c, :, columns:] = low

    total = wide_product(b_ref[0], pair[0], columns)
    for c in range(1, clients):
        total = total + wide_product(b_ref[c], pair[c], columns)
    for k in range(pl.num_programs(0)):

        @pl.when(step == k)
        def _():
            refs[k][...] = total


def panel_terms(b_factors, mine, partner, where, half, ranks, blocks, squares):
    clients, rows, slots = b_factors.shape
    columns = mine.shape[1]
    tall = rows // blocks
    outs = [jax.ShapeDtypeStruct((tall, columns), F32)] * blocks
    if squares:
        outs = outs + [jax.ShapeDtypeStruct((EXTRA, columns), F32)]
    whole = lambda array: pl.BlockSpec(array.shape, lambda step, where, half, ranks: (0, 0))
    return pl.pallas_call(
        functools.partial(panel_kernel, squares),
        grid_spec=pltpu.PrefetchScalarGridSpec(
            num_scalar_prefetch=3,
            grid=(blocks,),
            in_specs=[
                pl.BlockSpec((clients, tall, slots), lambda step, where, half, ranks: (0, where[step], 0)),
                whole(mine),
                whole(partner),
            ],
            out_specs=[whole(out) for out in outs],
            scratch_shapes=[pltpu.VMEM((clients, slots, 2 * columns), BF16)],
        ),
        out_shape=outs,
        compiler_params=params(32),
        cost_estimate=cost(8 * clients * slots * rows * columns, 4 * clients * slots * rows),
        name="panel",
    )(where, half, ranks, b_factors, mine, partner)


def gram_kernel(blocks, where, half, *refs):
    inputs, (other, mine), (highs, lows) = refs[: GROUPS * blocks], refs[-4:-2], refs[-2:]
    rows, columns = inputs[0].shape
    for g in range(GROUPS):
        for k in range(blocks):
            high, low = split(inputs[g * blocks + k][...])
            at = pl.ds(pl.multiple_of(where[k] * rows, rows), rows)
            highs[at, g * columns : (g + 1) * columns] = high
            lows[at, g * columns : (g + 1) * columns] = low
    contract = (((0,), (0,)), ((), ()))
    high = highs[...]
    cross = lax.dot_general(high, lows[...], contract, preferred_element_type=F32)
    gram = lax.dot_general(high, high, contract, preferred_element_type=F32) + (cross + cross.T)
    tall = other.shape[0]
    first = half[0] == 0
    other[...] = jnp.where(first, gram[tall:], gram[:tall])
    mine[...] = jnp.where(first, gram[:tall], gram[tall:])


def gram_terms(panels, where, half):
    blocks = len(panels[0])
    rows, columns = panels[0][0].shape
    size = GROUPS * columns
    smem = pl.BlockSpec(memory_space=pltpu.SMEM)
    return pl.pallas_call(
        functools.partial(gram_kernel, blocks),
        in_specs=[smem, smem] + [WHOLE] * (GROUPS * blocks),
        out_specs=[WHOLE] * 2,
        out_shape=[jax.ShapeDtypeStruct((size // 2, size), F32)] * 2,
        scratch_shapes=[pltpu.VMEM((blocks * rows, size), BF16)] * 2,
        compiler_params=params(32),
        cost_estimate=cost(4 * blocks * rows * size * size, 4 * blocks * rows * size),
        name="gram",
    )(where, half, *[block for panel in panels for block in panel])


def iterate(gram):
    size = gram.shape[0]
    row = lax.broadcasted_iota(jnp.int32, gram.shape, 0)
    column = lax.broadcasted_iota(jnp.int32, gram.shape, 1)
    eye = jnp.where(row == column, 1.0, 0.0).astype(F32)
    trace = jnp.sum(jnp.sum(gram * eye, axis=0, keepdims=True), axis=1, keepdims=True)
    scale = lax.rsqrt(trace)
    inner = gram * scale * scale
    mixing = None
    for turn in range(NS_STEPS):
        factor = 1.5 * eye - 0.5 * inner
        mixing = product(mixing, factor) if turn else factor * scale
        if turn < NS_STEPS - 1:
            inner = product(product(inner, factor), factor)
    return mixing


def joined(half, mine, partner):
    first = half[0] == 0
    low = jnp.where(first, mine[...], partner[...])
    high = jnp.where(first, partner[...], mine[...])
    return jnp.concatenate([low, high], axis=0)


def first_kernel(half, mine, partner, out):
    out[...] = iterate(joined(half, mine, partner))


def next_kernel(factor, half, mine, partner, before, *refs):
    scales, out = refs[:-1], refs[-1]
    columns = scales[0].shape[1]
    mixing = jnp.concatenate(
        [before[g * columns : (g + 1) * columns, :] / scales[g][0:1, 0:1] for g in range(GROUPS)], axis=0
    )
    gram = joined(half, mine, partner)
    out[...] = product(mixing, iterate(product(mixing.T, product(gram, mixing)))) * factor


def mixing_of(half, mine, partner, before=None, scales=(), factor=1.0):
    size = mine.shape[1]
    smem = pl.BlockSpec(memory_space=pltpu.SMEM)
    operands = (half, mine, partner) + (() if before is None else (before,) + tuple(scales))
    return pl.pallas_call(
        first_kernel if before is None else functools.partial(next_kernel, factor),
        in_specs=[smem] + [WHOLE] * (len(operands) - 1),
        out_specs=WHOLE,
        out_shape=jax.ShapeDtypeStruct((size, size), F32),
        compiler_params=params(32),
        cost_estimate=cost(90 * size**3, 12 * size * size),
        name="mixing",
    )(*operands)


def apply_kernel(blocks, where, mixing, *refs):
    inputs, (out,) = refs[: GROUPS * blocks], refs[GROUPS * blocks :]
    rows, columns = inputs[0].shape
    high, low = split(mixing[...])
    for k in range(blocks):
        value = jnp.concatenate([inputs[g * blocks + k][...] for g in range(GROUPS)], axis=1)
        value_high, value_low = split(value)
        at = pl.ds(pl.multiple_of(where[k] * rows, rows), rows)
        out[at, :] = dot(value_high, high) + (dot(value_high, low) + dot(value_low, high))


def apply_mixing(panels, where, mixing):
    blocks = len(panels[0])
    rows, columns = panels[0][0].shape
    size = GROUPS * columns
    smem = pl.BlockSpec(memory_space=pltpu.SMEM)
    return pl.pallas_call(
        functools.partial(apply_kernel, blocks),
        in_specs=[smem] + [WHOLE] * (1 + GROUPS * blocks),
        out_specs=WHOLE,
        out_shape=jax.ShapeDtypeStruct((blocks * rows, size), F32),
        compiler_params=params(32),
        cost_estimate=cost(6 * blocks * rows * size * size, 8 * blocks * rows * size),
        name="apply",
    )(where, mixing, *[block for panel in panels for block in panel])


class Grid:
    def __init__(self, mesh):
        self.cohorts = mesh.shape["cohort"]
        self.feats = mesh.shape["feat"]
        self.places = self.cohorts // 2
        cohort = lax.axis_index("cohort")
        place, side = cohort // 2, cohort % 2
        self.half = (lax.axis_index("feat") % 2).astype(jnp.int32).reshape(1)

        def block(step, side):
            return lax.rem(place - step + self.places, self.places) * 2 + side

        steps = range(self.places)
        self.scatter_order = jnp.stack([block(s + 1, i) for s in steps for i in (1 - side, side)]).astype(jnp.int32)
        self.gather_order = jnp.stack([block(s, i) for s in steps for i in (side, 1 - side)]).astype(jnp.int32)

    def across(self, block):
        return lax.ppermute(block, "cohort", [(i, i ^ 1) for i in range(self.cohorts)])

    def along(self, block):
        return lax.ppermute(block, "cohort", [(i, (i + 2) % self.cohorts) for i in range(self.cohorts)])

    def feat_swap(self, block, bit):
        return lax.ppermute(block, "feat", [(i, i ^ bit) for i in range(self.feats)])

    def feat_sum(self, other, mine):
        total = mine + self.feat_swap(other, 1)
        bit = 2
        while bit < self.feats:
            total = total + self.feat_swap(total, bit)
            bit *= 2
        return total, self.feat_swap(total, 1)

    def scatter_sum(self, blocks):
        total, arrived = None, []
        for step in range(self.places):
            send, keep = blocks[2 * step], blocks[2 * step + 1]
            if step > 1:
                send, arrived[step - 2] = lax.optimization_barrier((send, arrived[step - 2]))
            arrived.append(self.across(send))
        for step in range(self.places):
            fresh = arrived[step] + blocks[2 * step + 1]
            total = fresh if total is None else fresh + self.along(total)
        return total

    def gather(self, block):
        blocks = []
        for step in range(self.places):
            blocks += [block, self.across(block)]
            if step < self.places - 1:
                block = self.along(block)
        return blocks


def solution(mesh):
    def on_device(b_factors, a_factors, ranks, probes):
        grid = Grid(mesh)
        clients, rows, slots = b_factors.shape
        a_rows = a_factors.reshape(clients * slots, rows)
        origin = jnp.zeros((1,), jnp.int32)
        mixing = None
        for turn in range(ITERS):
            squares = turn > 0
            if turn == 0:
                halves = coef_terms(a_rows, [probes], origin, grid.half, GROUPS, squares)
                halves = [halves[2 * g : 2 * g + 2] for g in range(GROUPS)]
            panels, scales = [], []
            for g in range(GROUPS):
                if turn > 0:
                    halves[g] = coef_terms(a_rows, before[g], grid.gather_order, grid.half, 1, squares)
                mine, partner = grid.feat_sum(*halves[g])
                terms = panel_terms(
                    b_factors, mine, partner, grid.scatter_order, grid.half, ranks, grid.cohorts, squares
                )
                scales += terms[grid.cohorts :]
                panels.append(grid.gather(grid.scatter_sum(terms[: grid.cohorts])))
            gram = grid.feat_sum(*gram_terms(panels, grid.gather_order, grid.half))
            if turn == 0:
                mixing = mixing_of(grid.half, *gram)
            else:
                last = turn == ITERS - 1
                factor = math.sqrt(rows * grid.feats) if last else 1.0
                mixing = mixing_of(grid.half, *gram, mixing, scales, factor)
            before = panels
        return apply_mixing(panels, grid.gather_order, mixing)

    in_specs = (P("cohort", "feat", None), P("cohort", None, "feat"), P("cohort"), P("feat", None))
    return jax.shard_map(on_device, mesh=mesh, in_specs=in_specs, out_specs=P("feat", None), check_vma=False)
```

```python
import functools
import math

import jax
import jax.numpy as jnp
from jax import lax
from jax.experimental import pallas as pl
from jax.experimental.pallas import tpu as pltpu
from jax.sharding import PartitionSpec as P

ITERS = 2
NS_STEPS = 5
GROUPS = 2
EXTRA = 8
SLICES = 4
LARGE = 16
RING_SCATTER = True
RING_GATHER = True
CHAIN = 2
SCATTER_CHAIN = 2
ORDER_FEAT = 1
ORDER_SCATTER = 0
ORDER_GATHER = 0
JOIN = 1
WHOLE = pl.BlockSpec(memory_space=pltpu.VMEM)
SCALARS = pl.BlockSpec(memory_space=pltpu.SMEM)
F32 = jnp.float32
BF16 = jnp.bfloat16


def split(value):
    high = value.astype(BF16)
    return high, (value - high.astype(F32)).astype(BF16)


def dot(left, right):
    return jnp.dot(left, right, preferred_element_type=F32)


def product(left, right):
    left_high, left_low = split(left)
    right_high, right_low = split(right)
    return dot(left_high, right_high) + (dot(left_high, right_low) + dot(left_low, right_high))


def wide_product(left, pair, width):
    high, low = split(left)
    both = dot(high, pair)
    return both[:, :width] + (both[:, width:] + dot(low, pair[:, :width]))


def params(mib):
    return pltpu.CompilerParams(vmem_limit_bytes=mib * 2**20)


def cost(flops, moved):
    return pl.CostEstimate(flops=int(flops), bytes_accessed=int(moved), transcendentals=0)


def accumulate(a_ref, pair, total, columns):
    depth = a_ref.shape[1]
    wide = depth // SLICES
    for k in range(SLICES):
        at = pl.ds(k * wide, wide)
        term = wide_product(a_ref[:, at], pair[at, :], columns)
        total[...] = total[...] + term if k else term


def hand_out(total, half, outputs):
    tall = total.shape[0] // 2
    for out, at in zip(outputs, [(1 - half[0]) * tall, half[0] * tall]):
        out[:tall, :] = total[pl.ds(pl.multiple_of(at, tall), tall), :]


def first_coef_kernel(group, half, probes, a_ref, *refs):
    outputs, (pair, total) = refs[-4:-2], refs[-2:]
    columns = total.shape[1]
    high, low = split(probes[:, group * columns : (group + 1) * columns])
    pair[:, :columns] = high
    pair[:, columns:] = low
    accumulate(a_ref, pair, total, columns)
    hand_out(total, half, outputs)


def first_coef(a_rows, probes, group, half, also):
    total, depth = a_rows.shape
    columns = probes.shape[1] // GROUPS
    return pl.pallas_call(
        functools.partial(first_coef_kernel, group),
        in_specs=[SCALARS] + [WHOLE] * (2 + len(also)),
        out_specs=[WHOLE] * 2,
        out_shape=[jax.ShapeDtypeStruct((total // 2, columns), F32)] * 2,
        scratch_shapes=[
            pltpu.VMEM((depth, 2 * columns), BF16),
            pltpu.VMEM((total, columns), F32),
        ],
        compiler_params=params(LARGE),
        cost_estimate=cost(8 * total * depth * columns, 4 * total * depth),
        name="first_coef",
    )(half, probes, a_rows, *also)


def coef_kernel(blocks, where, half, a_ref, *refs):
    inputs, outputs, (pair, total, sums) = refs[:blocks], refs[blocks:-3], refs[-3:]
    rows, columns = inputs[0].shape
    for k in range(blocks):
        value = inputs[k][...]
        high, low = split(value)
        at = pl.ds(pl.multiple_of(where[k] * rows, rows), rows)
        pair[at, :columns] = high
        pair[at, columns:] = low
        sums[pl.ds(where[k], 1), :] = jnp.sum(value * value, axis=0, keepdims=True)
    square = jnp.sum(sums[...], axis=0, keepdims=True)
    square = jnp.sum(square, axis=1, keepdims=True)
    for out in outputs:
        out[out.shape[0] - EXTRA :, :] = jnp.broadcast_to(square, (EXTRA, out.shape[1]))
    accumulate(a_ref, pair, total, columns)
    hand_out(total, half, outputs)


def coef_terms(a_rows, basis, where, half):
    total, depth = a_rows.shape
    columns = basis[0].shape[1]
    return pl.pallas_call(
        functools.partial(coef_kernel, len(basis)),
        in_specs=[SCALARS, SCALARS, WHOLE] + [WHOLE] * len(basis),
        out_specs=[WHOLE] * 2,
        out_shape=[jax.ShapeDtypeStruct((total // 2 + EXTRA, columns), F32)] * 2,
        scratch_shapes=[
            pltpu.VMEM((depth, 2 * columns), BF16),
            pltpu.VMEM((total, columns), F32),
            pltpu.VMEM((len(basis), columns), F32),
        ],
        compiler_params=params(LARGE),
        cost_estimate=cost(8 * total * depth * columns, 4 * total * depth),
        name="coef",
    )(where, half, a_rows, *basis)


def panel_kernel(sizes, squares, where, half, ranks, b_ref, mine_ref, partner_ref, *refs):
    total = refs[-1]
    clients, rows, slots = b_ref.shape
    columns = total.shape[1]
    scale = jnp.ones((1, columns), F32)
    if squares:
        square = mine_ref[mine_ref.shape[0] - EXTRA : mine_ref.shape[0] - EXTRA + 1, :]
        scale = jnp.where(square > 0, lax.rsqrt(square), 1.0)
        refs[len(sizes)][...] = jnp.broadcast_to(scale, refs[len(sizes)].shape)
    first = half[0] == 0
    for c in range(clients):
        at = pl.ds((c % (clients // 2)) * slots, slots)
        mine, partner = mine_ref[at, :], partner_ref[at, :]
        value = jnp.where(first, mine, partner) if c < clients // 2 else jnp.where(first, partner, mine)
        slot = lax.broadcasted_iota(jnp.int32, value.shape, 0)
        value = jnp.where(slot < ranks[c], value * scale, 0.0)
        term = wide_product(b_ref[c], jnp.concatenate(split(value), axis=1), columns)
        total[...] = total[...] + term if c else term
    tall = rows // sum(sizes)
    k = 0
    for out, size in zip(refs, sizes):
        for i in range(size):
            out[i * tall : (i + 1) * tall, :] = total[pl.ds(pl.multiple_of(where[k] * tall, tall), tall), :]
            k += 1


def panel_terms(b_factors, mine, partner, where, half, ranks, sizes, squares):
    clients, rows, slots = b_factors.shape
    columns = mine.shape[1]
    tall = rows // sum(sizes)
    outs = [jax.ShapeDtypeStruct((size * tall, columns), F32) for size in sizes]
    if squares:
        outs = outs + [jax.ShapeDtypeStruct((EXTRA, columns), F32)]
    return pl.pallas_call(
        functools.partial(panel_kernel, sizes, squares),
        in_specs=[SCALARS] * 3 + [WHOLE] * 3,
        out_specs=[WHOLE] * len(outs),
        out_shape=outs,
        scratch_shapes=[
            pltpu.VMEM((rows, columns), F32),
        ],
        compiler_params=params(LARGE),
        cost_estimate=cost(8 * clients * slots * rows * columns, 4 * clients * slots * rows),
        name="panel",
    )(where, half, ranks, b_factors, mine, partner)


def gram_kernel(blocks, where, half, *refs):
    inputs, (other, mine), (highs, lows) = refs[: GROUPS * blocks], refs[-4:-2], refs[-2:]
    rows, columns = inputs[0].shape
    for g in range(GROUPS):
        for k in range(blocks):
            high, low = split(inputs[g * blocks + k][...])
            at = pl.ds(pl.multiple_of(where[k] * rows, rows), rows)
            highs[at, g * columns : (g + 1) * columns] = high
            lows[at, g * columns : (g + 1) * columns] = low
    contract = (((0,), (0,)), ((), ()))
    high = highs[...]
    cross = lax.dot_general(high, lows[...], contract, preferred_element_type=F32)
    gram = lax.dot_general(high, high, contract, preferred_element_type=F32) + (cross + cross.T)
    tall = other.shape[0]
    first = half[0] == 0
    other[...] = jnp.where(first, gram[tall:], gram[:tall])
    mine[...] = jnp.where(first, gram[:tall], gram[tall:])


def gram_terms(panels, where, half):
    blocks = len(panels[0])
    rows, columns = panels[0][0].shape
    size = GROUPS * columns
    return pl.pallas_call(
        functools.partial(gram_kernel, blocks),
        in_specs=[SCALARS, SCALARS] + [WHOLE] * (GROUPS * blocks),
        out_specs=[WHOLE] * 2,
        out_shape=[jax.ShapeDtypeStruct((size // 2, size), F32)] * 2,
        scratch_shapes=[pltpu.VMEM((blocks * rows, size), BF16)] * 2,
        compiler_params=params(LARGE),
        cost_estimate=cost(4 * blocks * rows * size * size, 4 * blocks * rows * size),
        name="gram",
    )(where, half, *[block for panel in panels for block in panel])


def iterate(gram):
    size = gram.shape[0]
    row = lax.broadcasted_iota(jnp.int32, gram.shape, 0)
    column = lax.broadcasted_iota(jnp.int32, gram.shape, 1)
    eye = jnp.where(row == column, 1.0, 0.0).astype(F32)
    trace = jnp.sum(jnp.sum(gram * eye, axis=0, keepdims=True), axis=1, keepdims=True)
    scale = lax.rsqrt(trace)
    inner = gram * scale * scale
    mixing = None
    for turn in range(NS_STEPS):
        factor = 1.5 * eye - 0.5 * inner
        mixing = product(mixing, factor) if turn else factor * scale
        if turn < NS_STEPS - 1:
            inner = product(product(inner, factor), factor)
    return mixing


def joined(half, mine, partner):
    first = half[0] == 0
    low = jnp.where(first, mine[...], partner[...])
    high = jnp.where(first, partner[...], mine[...])
    return jnp.concatenate([low, high], axis=0)


def first_kernel(half, mine, partner, out):
    out[...] = iterate(joined(half, mine, partner))


def next_kernel(factor, half, mine, partner, before, *refs):
    scales, out = refs[:-1], refs[-1]
    columns = scales[0].shape[1]
    mixing = jnp.concatenate(
        [before[g * columns : (g + 1) * columns, :] / scales[g][0:1, 0:1] for g in range(GROUPS)], axis=0
    )
    gram = joined(half, mine, partner)
    out[...] = product(mixing, iterate(product(mixing.T, product(gram, mixing)))) * factor


def mixing_of(half, mine, partner, before=None, scales=(), factor=1.0):
    size = mine.shape[1]
    operands = (half, mine, partner) + (() if before is None else (before,) + tuple(scales))
    return pl.pallas_call(
        first_kernel if before is None else functools.partial(next_kernel, factor),
        in_specs=[SCALARS] + [WHOLE] * (len(operands) - 1),
        out_specs=WHOLE,
        out_shape=jax.ShapeDtypeStruct((size, size), F32),
        compiler_params=params(LARGE),
        cost_estimate=cost(90 * size**3, 12 * size * size),
        name="mixing",
    )(*operands)


def apply_kernel(blocks, where, mixing, *refs):
    inputs, (out,) = refs[: GROUPS * blocks], refs[GROUPS * blocks :]
    rows, columns = inputs[0].shape
    high, low = split(mixing[...])
    for k in range(blocks):
        value = jnp.concatenate([inputs[g * blocks + k][...] for g in range(GROUPS)], axis=1)
        value_high, value_low = split(value)
        at = pl.ds(pl.multiple_of(where[k] * rows, rows), rows)
        out[at, :] = dot(value_high, high) + (dot(value_high, low) + dot(value_low, high))


def apply_mixing(panels, where, mixing):
    blocks = len(panels[0])
    rows, columns = panels[0][0].shape
    size = GROUPS * columns
    return pl.pallas_call(
        functools.partial(apply_kernel, blocks),
        in_specs=[SCALARS] + [WHOLE] * (1 + GROUPS * blocks),
        out_specs=WHOLE,
        out_shape=jax.ShapeDtypeStruct((blocks * rows, size), F32),
        compiler_params=params(LARGE),
        cost_estimate=cost(6 * blocks * rows * size * size, 8 * blocks * rows * size),
        name="apply",
    )(where, mixing, *[block for panel in panels for block in panel])


class Grid:
    def __init__(self, mesh, go):
        self.go = go
        self.cohorts = mesh.shape["cohort"]
        self.feats = mesh.shape["feat"]
        self.places = self.cohorts // 2
        cohort = lax.axis_index("cohort")
        place, side = cohort // 2, cohort % 2
        self.half = (lax.axis_index("feat") % 2).astype(jnp.int32).reshape(1)
        shifts = sorted(range(1, self.places), key=lambda d: (-min(d, self.places - d), d)) + [0]
        self.out_shifts = list(range(-1, -self.places, -1)) + [0] if RING_SCATTER else shifts
        self.in_shifts = list(range(0, -self.places, -1)) if RING_GATHER else [-d for d in shifts[::-1]]

        def block(shift, side):
            return lax.rem(place + shift + self.places, self.places) * 2 + side

        self.sendings = [self.out_shifts[i : i + JOIN] for i in range(0, self.places, JOIN)]
        self.sizes = [len(s) for s in self.sendings] + [1] * self.places
        self.scatter_order = jnp.stack(
            [block(d, 1 - side) for d in self.out_shifts] + [block(d, side) for d in self.out_shifts]
        ).astype(jnp.int32)
        self.gather_order = jnp.stack([block(d, s) for d in self.in_shifts for s in (side, 1 - side)]).astype(jnp.int32)

    def across(self, block):
        return lax.ppermute(block, "cohort", [(i, i ^ 1) for i in range(self.cohorts)])

    def along(self, block, shift):
        return lax.ppermute(block, "cohort", [(i, (i + 2 * shift) % self.cohorts) for i in range(self.cohorts)])

    def feat_swap(self, block, bit):
        return lax.ppermute(block, "feat", [(i, i ^ bit) for i in range(self.feats)])

    def feat_sum(self, other, mine, after=None):
        total = mine + self.feat_swap(other, 1)
        if after is not None:
            total = self.follow(total, after)
        bit = 2
        while bit < self.feats:
            total = total + self.feat_swap(total, bit)
            bit *= 2
        return total, self.feat_swap(total, 1)

    def follow(self, block, earlier):
        return jnp.where(self.go, block, earlier[: block.shape[0], : block.shape[1]])

    def scatter_sum(self, terms, after=None):
        keep = terms[len(self.sendings) :]
        rows = keep[0].shape[0]
        total, arrivals = None, []
        for i, sending in enumerate(self.sendings):
            send = terms[i]
            if SCATTER_CHAIN and i >= SCATTER_CHAIN:
                send = self.follow(send, arrivals[i - SCATTER_CHAIN])
            elif after is not None:
                send = self.follow(send, after)
            arrived = self.across(send)
            arrivals.append(arrived)
            for j, shift in enumerate(sending):
                here = arrived[j * rows : (j + 1) * rows] + keep[JOIN * i + j]
                if RING_SCATTER:
                    total = here if total is None else here + self.along(total, 1)
                else:
                    here = self.along(here, shift) if shift else here
                    total = here if total is None else total + here
        return total, arrivals

    def gather(self, block, early=None, after=None):
        blocks = []
        if after is not None:
            block = self.follow(block, after)
        own = block
        for step, shift in enumerate(self.in_shifts):
            if step and RING_GATHER:
                if CHAIN and step >= CHAIN:
                    block = self.follow(block, blocks[2 * (step - CHAIN) + 1])
                block = self.along(block, 1)
            elif step:
                block = self.along(own, -shift)
            if early is not None and step == self.places - 1:
                block = self.follow(block, early)
            blocks += [block, self.across(block)]
        return blocks


def solution(mesh):
    def on_device(b_factors, a_factors, ranks, probes):
        grid = Grid(mesh, ranks[0] > 0)
        clients, rows, slots = b_factors.shape
        a_rows = a_factors.reshape(clients * slots, rows)
        mixing, panels = None, None
        for turn in range(ITERS):
            squares = turn > 0
            if turn == 0:
                halves = [first_coef(a_rows, probes, g, grid.half, [b_factors] if g else []) for g in range(GROUPS)]
            else:
                halves = [coef_terms(a_rows, panel, grid.gather_order, grid.half) for panel in panels]
            totals, scales, arrivals, mine = [], [], None, None
            for g in range(GROUPS):
                mine, partner = grid.feat_sum(*halves[g], mine if ORDER_FEAT else None)
                terms = panel_terms(
                    b_factors, mine, partner, grid.scatter_order, grid.half, ranks, grid.sizes, squares
                )
                scales += terms[len(grid.sizes) :]
                after = arrivals[ORDER_SCATTER] if g and ORDER_SCATTER else None
                total, arrivals = grid.scatter_sum(terms[: len(grid.sizes)], after)
                totals.append(total)
            panels = []
            for g in range(GROUPS):
                after = panels[-1][ORDER_GATHER] if g and ORDER_GATHER else None
                panels.append(grid.gather(totals[g], mixing if g else None, after))
            gram = grid.feat_sum(*gram_terms(panels, grid.gather_order, grid.half))
            if turn == 0:
                mixing = mixing_of(grid.half, *gram)
            else:
                last = turn == ITERS - 1
                factor = math.sqrt(rows * grid.feats) if last else 1.0
                mixing = mixing_of(grid.half, *gram, mixing, scales, factor)
        return apply_mixing(panels, grid.gather_order, mixing)

    in_specs = (P("cohort", "feat", None), P("cohort", None, "feat"), P("cohort"), P("feat", None))
    return jax.shard_map(on_device, mesh=mesh, in_specs=in_specs, out_specs=P("feat", None), check_vma=False)
```

```python
import functools
import math

import jax
import jax.numpy as jnp
from jax import lax
from jax.experimental import pallas as pl
from jax.experimental.pallas import tpu as pltpu
from jax.sharding import PartitionSpec as P

ITERS = 2
NS_STEPS = 5
GROUPS = 2
EXTRA = 8
SLICES = 4
LARGE = 16
HOLD = 1
FIRST_OUT = 2
NEXT_OUT = 2
NEXT_IN = 2
PANELS_FIRST = 0
SWAP_GATE = 1
IN_TURN = 1
LATE_GRAM = 1
WHOLE = pl.BlockSpec(memory_space=pltpu.VMEM)
SCALARS = pl.BlockSpec(memory_space=pltpu.SMEM)
F32 = jnp.float32
BF16 = jnp.bfloat16


def split(value):
    high = value.astype(BF16)
    return high, (value - high.astype(F32)).astype(BF16)


def dot(left, right):
    return jnp.dot(left, right, preferred_element_type=F32)


def product(left, right):
    left_high, left_low = split(left)
    right_high, right_low = split(right)
    return dot(left_high, right_high) + (dot(left_high, right_low) + dot(left_low, right_high))


def wide_product(left, pair, width):
    high, low = split(left)
    both = dot(high, pair)
    return both[:, :width] + (both[:, width:] + dot(low, pair[:, :width]))


def params(mib):
    return pltpu.CompilerParams(vmem_limit_bytes=mib * 2**20)


def cost(flops, moved):
    return pl.CostEstimate(flops=int(flops), bytes_accessed=int(moved), transcendentals=0)


def accumulate(a_ref, pair, total, columns):
    depth = a_ref.shape[1]
    wide = depth // SLICES
    for k in range(SLICES):
        at = pl.ds(k * wide, wide)
        term = wide_product(a_ref[:, at], pair[at, :], columns)
        total[...] = total[...] + term if k else term


def hand_out(total, half, outputs):
    tall = total.shape[0] // 2
    for out, at in zip(outputs, [(1 - half[0]) * tall, half[0] * tall]):
        out[:tall, :] = total[pl.ds(pl.multiple_of(at, tall), tall), :]


def first_coef_kernel(group, half, probes, a_ref, *refs):
    outputs, (pair, total) = refs[-4:-2], refs[-2:]
    columns = total.shape[1]
    high, low = split(probes[:, group * columns : (group + 1) * columns])
    pair[:, :columns] = high
    pair[:, columns:] = low
    accumulate(a_ref, pair, total, columns)
    hand_out(total, half, outputs)


def first_coef(a_rows, probes, group, half, also):
    total, depth = a_rows.shape
    columns = probes.shape[1] // GROUPS
    return pl.pallas_call(
        functools.partial(first_coef_kernel, group),
        in_specs=[SCALARS] + [WHOLE] * (2 + len(also)),
        out_specs=[WHOLE] * 2,
        out_shape=[jax.ShapeDtypeStruct((total // 2, columns), F32)] * 2,
        scratch_shapes=[
            pltpu.VMEM((depth, 2 * columns), BF16),
            pltpu.VMEM((total, columns), F32),
        ],
        compiler_params=params(LARGE),
        cost_estimate=cost(8 * total * depth * columns, 4 * total * depth),
        name="first_coef",
    )(half, probes, a_rows, *also)


def pieces(inputs, rows):
    return [ref[i : i + rows, :] for ref in inputs for i in range(0, ref.shape[0], rows)]


def coef_kernel(rows, where, half, a_ref, *refs):
    inputs, outputs, (pair, total, sums) = refs[:-5], refs[-5:-3], refs[-3:]
    columns = inputs[0].shape[1]
    for k, value in enumerate(pieces(inputs, rows)):
        high, low = split(value)
        at = pl.ds(pl.multiple_of(where[k] * rows, rows), rows)
        pair[at, :columns] = high
        pair[at, columns:] = low
        sums[pl.ds(where[k], 1), :] = jnp.sum(value * value, axis=0, keepdims=True)
    square = jnp.sum(sums[...], axis=0, keepdims=True)
    square = jnp.sum(square, axis=1, keepdims=True)
    for out in outputs:
        out[out.shape[0] - EXTRA :, :] = jnp.broadcast_to(square, (EXTRA, out.shape[1]))
    accumulate(a_ref, pair, total, columns)
    hand_out(total, half, outputs)


def coef_terms(a_rows, basis, where, half):
    total, depth = a_rows.shape
    columns = basis[0].shape[1]
    return pl.pallas_call(
        functools.partial(coef_kernel, depth // where.shape[0]),
        in_specs=[SCALARS, SCALARS, WHOLE] + [WHOLE] * len(basis),
        out_specs=[WHOLE] * 2,
        out_shape=[jax.ShapeDtypeStruct((total // 2 + EXTRA, columns), F32)] * 2,
        scratch_shapes=[
            pltpu.VMEM((depth, 2 * columns), BF16),
            pltpu.VMEM((total, columns), F32),
            pltpu.VMEM((where.shape[0], columns), F32),
        ],
        compiler_params=params(LARGE),
        cost_estimate=cost(8 * total * depth * columns, 4 * total * depth),
        name="coef",
    )(where, half, a_rows, *basis)


def panel_kernel(sizes, squares, where, half, ranks, b_ref, mine_ref, partner_ref, *refs):
    total = refs[-1]
    clients, rows, slots = b_ref.shape
    columns = total.shape[1]
    scale = jnp.ones((1, columns), F32)
    if squares:
        square = mine_ref[mine_ref.shape[0] - EXTRA : mine_ref.shape[0] - EXTRA + 1, :]
        scale = jnp.where(square > 0, lax.rsqrt(square), 1.0)
        refs[len(sizes)][...] = jnp.broadcast_to(scale, refs[len(sizes)].shape)
    first = half[0] == 0
    for c in range(clients):
        at = pl.ds((c % (clients // 2)) * slots, slots)
        mine, partner = mine_ref[at, :], partner_ref[at, :]
        value = jnp.where(first, mine, partner) if c < clients // 2 else jnp.where(first, partner, mine)
        slot = lax.broadcasted_iota(jnp.int32, value.shape, 0)
        value = jnp.where(slot < ranks[c], value * scale, 0.0)
        term = wide_product(b_ref[c], jnp.concatenate(split(value), axis=1), columns)
        total[...] = total[...] + term if c else term
    tall = rows // sum(sizes)
    k = 0
    for out, size in zip(refs, sizes):
        for i in range(size):
            out[i * tall : (i + 1) * tall, :] = total[pl.ds(pl.multiple_of(where[k] * tall, tall), tall), :]
            k += 1


def panel_terms(b_factors, mine, partner, where, half, ranks, sizes, squares):
    clients, rows, slots = b_factors.shape
    columns = mine.shape[1]
    tall = rows // sum(sizes)
    outs = [jax.ShapeDtypeStruct((size * tall, columns), F32) for size in sizes]
    if squares:
        outs = outs + [jax.ShapeDtypeStruct((EXTRA, columns), F32)]
    return pl.pallas_call(
        functools.partial(panel_kernel, sizes, squares),
        in_specs=[SCALARS] * 3 + [WHOLE] * 3,
        out_specs=[WHOLE] * len(outs),
        out_shape=outs,
        scratch_shapes=[
            pltpu.VMEM((rows, columns), F32),
        ],
        compiler_params=params(LARGE),
        cost_estimate=cost(8 * clients * slots * rows * columns, 4 * clients * slots * rows),
        name="panel",
    )(where, half, ranks, b_factors, mine, partner)


def gram_kernel(rows, where, half, *refs):
    inputs, (other, mine), (highs, lows) = refs[:-4], refs[-4:-2], refs[-2:]
    columns = inputs[0].shape[1]
    each = len(inputs) // GROUPS
    for g in range(GROUPS):
        for k, value in enumerate(pieces(inputs[g * each : (g + 1) * each], rows)):
            high, low = split(value)
            at = pl.ds(pl.multiple_of(where[k] * rows, rows), rows)
            highs[at, g * columns : (g + 1) * columns] = high
            lows[at, g * columns : (g + 1) * columns] = low
    contract = (((0,), (0,)), ((), ()))
    high = highs[...]
    cross = lax.dot_general(high, lows[...], contract, preferred_element_type=F32)
    gram = lax.dot_general(high, high, contract, preferred_element_type=F32) + (cross + cross.T)
    tall = other.shape[0]
    first = half[0] == 0
    other[...] = jnp.where(first, gram[tall:], gram[:tall])
    mine[...] = jnp.where(first, gram[:tall], gram[tall:])


def gram_terms(panels, where, half):
    blocks = where.shape[0]
    rows, columns = panels[0][0].shape
    size = GROUPS * columns
    return pl.pallas_call(
        functools.partial(gram_kernel, rows),
        in_specs=[SCALARS, SCALARS] + [WHOLE] * sum(len(panel) for panel in panels),
        out_specs=[WHOLE] * 2,
        out_shape=[jax.ShapeDtypeStruct((size // 2, size), F32)] * 2,
        scratch_shapes=[pltpu.VMEM((blocks * rows, size), BF16)] * 2,
        compiler_params=params(LARGE),
        cost_estimate=cost(4 * blocks * rows * size * size, 4 * blocks * rows * size),
        name="gram",
    )(where, half, *[block for panel in panels for block in panel])


def iterate(gram):
    size = gram.shape[0]
    row = lax.broadcasted_iota(jnp.int32, gram.shape, 0)
    column = lax.broadcasted_iota(jnp.int32, gram.shape, 1)
    eye = jnp.where(row == column, 1.0, 0.0).astype(F32)
    trace = jnp.sum(jnp.sum(gram * eye, axis=0, keepdims=True), axis=1, keepdims=True)
    scale = lax.rsqrt(trace)
    inner = gram * scale * scale
    mixing = None
    for turn in range(NS_STEPS):
        factor = 1.5 * eye - 0.5 * inner
        mixing = product(mixing, factor) if turn else factor * scale
        if turn < NS_STEPS - 1:
            inner = product(product(inner, factor), factor)
    return mixing


def joined(half, mine, partner):
    first = half[0] == 0
    low = jnp.where(first, mine[...], partner[...])
    high = jnp.where(first, partner[...], mine[...])
    return jnp.concatenate([low, high], axis=0)


def first_kernel(half, mine, partner, out):
    out[...] = iterate(joined(half, mine, partner))


def next_kernel(factor, half, mine, partner, before, *refs):
    scales, out = refs[:-1], refs[-1]
    columns = scales[0].shape[1]
    mixing = jnp.concatenate(
        [before[g * columns : (g + 1) * columns, :] / scales[g][0:1, 0:1] for g in range(GROUPS)], axis=0
    )
    gram = joined(half, mine, partner)
    out[...] = product(mixing, iterate(product(mixing.T, product(gram, mixing)))) * factor


def mixing_of(half, mine, partner, before=None, scales=(), factor=1.0):
    size = mine.shape[1]
    operands = (half, mine, partner) + (() if before is None else (before,) + tuple(scales))
    return pl.pallas_call(
        first_kernel if before is None else functools.partial(next_kernel, factor),
        in_specs=[SCALARS] + [WHOLE] * (len(operands) - 1),
        out_specs=WHOLE,
        out_shape=jax.ShapeDtypeStruct((size, size), F32),
        compiler_params=params(LARGE),
        cost_estimate=cost(90 * size**3, 12 * size * size),
        name="mixing",
    )(*operands)


def apply_kernel(rows, where, mixing, *refs):
    inputs, (out, held, sems) = refs[:-3], refs[-3:]
    each = len(inputs) // GROUPS
    high, low = split(mixing[...])
    copies = []
    values = [pieces(inputs[g * each : (g + 1) * each], rows) for g in range(GROUPS)]
    for k, value in enumerate(zip(*values)):
        value = jnp.concatenate(value, axis=1)
        value_high, value_low = split(value)
        held[k] = dot(value_high, high) + (dot(value_high, low) + dot(value_low, high))
        at = pl.ds(pl.multiple_of(where[k] * rows, rows), rows)
        copies.append(pltpu.make_async_copy(held.at[k], out.at[at], sems.at[k]))
        copies[k].start()
    for copy in copies:
        copy.wait()


def apply_mixing(panels, where, mixing):
    blocks = where.shape[0]
    rows, columns = panels[0][0].shape
    size = GROUPS * columns
    return pl.pallas_call(
        functools.partial(apply_kernel, rows),
        in_specs=[SCALARS] + [WHOLE] * (1 + sum(len(panel) for panel in panels)),
        out_specs=pl.BlockSpec(memory_space=pl.ANY),
        out_shape=jax.ShapeDtypeStruct((blocks * rows, size), F32),
        scratch_shapes=[pltpu.VMEM((blocks, rows, size), F32), pltpu.SemaphoreType.DMA((blocks,))],
        compiler_params=params(LARGE),
        cost_estimate=cost(6 * blocks * rows * size * size, 8 * blocks * rows * size),
        name="apply",
    )(where, mixing, *[block for panel in panels for block in panel])


class Grid:
    def __init__(self, mesh, go):
        self.go = go
        self.cohorts = mesh.shape["cohort"]
        self.feats = mesh.shape["feat"]
        self.places = self.cohorts // 2
        cohort = lax.axis_index("cohort")
        place, side = cohort // 2, cohort % 2
        self.half = (lax.axis_index("feat") % 2).astype(jnp.int32).reshape(1)
        def block(shift, side):
            return lax.rem(place + shift + self.places, self.places) * 2 + side

        ahead = self.places // 2
        self.shifts = sorted(range(ahead + 1 - self.places, ahead + 1), key=lambda d: (abs(d), -d))
        outward, inward = self.shifts[::-1], [-d for d in self.shifts]
        self.scatter_order = jnp.stack([block(d, s) for s in (1 - side, side) for d in outward]).astype(jnp.int32)
        self.gather_order = jnp.stack([block(d, s) for s in (side, 1 - side) for d in inward]).astype(jnp.int32)
        places = range(self.places)
        cuts = [0] + list(places)[FIRST_OUT :: NEXT_OUT] + [self.places]
        self.outs = [b - a for a, b in zip(cuts, cuts[1:])]
        self.sizes = self.outs + [1] * self.places
        cuts = [0] + list(places)[1::NEXT_IN] + [self.places]
        self.ins = list(zip(cuts, cuts[1:]))

    def across(self, block):
        return lax.ppermute(block, "cohort", [(i, i ^ 1) for i in range(self.cohorts)])

    def along(self, block, way):
        step = 2 if way > 0 else self.cohorts - 2
        return lax.ppermute(block, "cohort", [(i, (i + step) % self.cohorts) for i in range(self.cohorts)])

    def feat_swap(self, block, bit):
        return lax.ppermute(block, "feat", [(i, i ^ bit) for i in range(self.feats)])

    def feat_sum(self, other, mine, after=None, before_last=None):
        total = mine + self.feat_swap(other, 1)
        if after is not None:
            total = self.follow(total, after)
        bit = 2
        while bit < self.feats:
            total = total + self.feat_swap(total, bit)
            bit *= 2
        return total, self.feat_swap(total if before_last is None else self.follow(total, before_last), 1)

    def follow(self, block, earlier):
        rows, columns = (min(a, b) for a, b in zip(block.shape, earlier.shape))
        if rows < block.shape[0]:
            return jnp.concatenate([jnp.where(self.go, block[:rows], earlier[:rows, :columns]), block[rows:]], 0)
        return jnp.where(self.go, block, earlier[:rows, :columns])

    def scatter_sum(self, terms, early=None, turn=None):
        keep = terms[len(self.outs) :]
        rows = keep[0].shape[0]
        carried, step = {}, 0
        for i, size in enumerate(self.outs):
            send = terms[i]
            if i and early is not None:
                send = self.follow(send, early)
            if not i and turn is not None:
                send = self.follow(send, turn)
            arrived = self.across(send)
            if not i:
                arrival = arrived
            for j in range(size):
                shift = self.shifts[self.places - 1 - step]
                total = arrived[j * rows : (j + 1) * rows] + keep[step]
                step += 1
                way = (shift > 0) - (shift < 0)
                for carry in [carried.get(way)] if way else carried.values():
                    total = total if carry is None else total + carry
                if way:
                    carried[way] = self.along(total, way)
        return total, arrival

    def gather(self, block, early=None):
        carried = {0: block, 1: block, -1: block}
        near, far = [], []
        for first, end in self.ins:
            group = []
            for step in range(first, end):
                way = (self.shifts[step] > 0) - (self.shifts[step] < 0)
                if way:
                    if HOLD and step >= 3:
                        carried[way] = self.follow(carried[way], far[(step - 3) // NEXT_IN])
                    carried[way] = self.along(carried[way], way)
                group.append(carried[way])
            group = jnp.concatenate(group, 0) if len(group) > 1 else group[0]
            near.append(group)
            if early is not None and end == self.places:
                group = self.follow(group, early)
            far.append(self.across(group))
        return near + far


def solution(mesh):
    def on_device(b_factors, a_factors, ranks, probes):
        grid = Grid(mesh, ranks[0] > 0)
        clients, rows, slots = b_factors.shape
        a_rows = a_factors.reshape(clients * slots, rows)

        def mixing_after(mixing, panels, scales, factor):
            gram = grid.feat_sum(*gram_terms(panels, grid.gather_order, grid.half))
            return mixing_of(grid.half, *gram, mixing, scales if mixing is not None else (), factor)

        mixing, panels = None, None
        for turn in range(ITERS):
            squares = turn > 0
            if turn == 0:
                halves = [first_coef(a_rows, probes, g, grid.half, [b_factors] if g else []) for g in range(GROUPS)]
            else:
                halves = [coef_terms(a_rows, panel, grid.gather_order, grid.half) for panel in panels]
            terms, mine = [], None
            for g in range(GROUPS):
                before_last = terms[-1][0] if g and SWAP_GATE else None
                mine, partner = grid.feat_sum(*halves[g], mine, before_last)
                terms.append(
                    panel_terms(b_factors, mine, partner, grid.scatter_order, grid.half, ranks, grid.sizes, squares)
                )
            scales = [array for term in terms for array in term[len(grid.sizes) :]]
            terms = [term[: len(grid.sizes)] for term in terms]
            totals, arrival = [], None
            for g, term in enumerate(terms):
                early = terms[-1][-1] if g < GROUPS - 1 and PANELS_FIRST else None
                total, arrival = grid.scatter_sum(term, early, arrival if IN_TURN else None)
                totals.append(total)
            if turn:
                first = panels[0]
                if LATE_GRAM:
                    first = [grid.follow(first[0], totals[0])] + first[1:]
                mixing = mixing_after(mixing, [first] + panels[1:], before_scales, 1.0)
            panels = [grid.gather(total, mixing if g else None) for g, total in enumerate(totals)]
            before_scales = scales
        mixing = mixing_after(mixing, panels, scales, math.sqrt(rows * grid.feats))
        return apply_mixing(panels, grid.gather_order, mixing)

    in_specs = (P("cohort", "feat", None), P("cohort", None, "feat"), P("cohort"), P("feat", None))
    return jax.shard_map(on_device, mesh=mesh, in_specs=in_specs, out_specs=P("feat", None), check_vma=False)
```

```python
import functools
import math

import jax
import jax.numpy as jnp
from jax import lax
from jax.experimental import pallas as pl
from jax.experimental.pallas import tpu as pltpu
from jax.sharding import PartitionSpec as P

ITERS = 2
NS_STEPS = 5
GROUPS = 2
EXTRA = 8
SLICES = 4
LARGE = 16
HOLD = 1
FIRST_OUT = 2
NEXT_OUT = 2
NEXT_IN = 2
PANELS_FIRST = 0
SWAP_GATE = 1
IN_TURN = 1
LATE_GRAM = 1
WHOLE = pl.BlockSpec(memory_space=pltpu.VMEM)
SCALARS = pl.BlockSpec(memory_space=pltpu.SMEM)
F32 = jnp.float32
BF16 = jnp.bfloat16


def split(value):
    high = value.astype(BF16)
    return high, (value - high.astype(F32)).astype(BF16)


def dot(left, right):
    return jnp.dot(left, right, preferred_element_type=F32)


def product(left, right):
    left_high, left_low = split(left)
    right_high, right_low = split(right)
    return dot(left_high, right_high) + (dot(left_high, right_low) + dot(left_low, right_high))


def wide_product(left, pair, width):
    high, low = split(left)
    both = dot(high, pair)
    return both[:, :width] + (both[:, width:] + dot(low, pair[:, :width]))


def params(mib):
    return pltpu.CompilerParams(vmem_limit_bytes=mib * 2**20)


def cost(flops, moved):
    return pl.CostEstimate(flops=int(flops), bytes_accessed=int(moved), transcendentals=0)


def accumulate(a_ref, pair, total, columns):
    depth = a_ref.shape[1]
    wide = depth // SLICES
    for k in range(SLICES):
        at = pl.ds(k * wide, wide)
        term = wide_product(a_ref[:, at], pair[at, :], columns)
        total[...] = total[...] + term if k else term


def hand_out(total, half, outputs):
    tall = total.shape[0] // 2
    for out, at in zip(outputs, [(1 - half[0]) * tall, half[0] * tall]):
        out[:tall, :] = total[pl.ds(pl.multiple_of(at, tall), tall), :]


def first_coef_kernel(group, half, probes, a_ref, *refs):
    outputs, (pair, total) = refs[-4:-2], refs[-2:]
    columns = total.shape[1]
    high, low = split(probes[:, group * columns : (group + 1) * columns])
    pair[:, :columns] = high
    pair[:, columns:] = low
    accumulate(a_ref, pair, total, columns)
    hand_out(total, half, outputs)


def first_coef(a_rows, probes, group, half, also):
    total, depth = a_rows.shape
    columns = probes.shape[1] // GROUPS
    return pl.pallas_call(
        functools.partial(first_coef_kernel, group),
        in_specs=[SCALARS] + [WHOLE] * (2 + len(also)),
        out_specs=[WHOLE] * 2,
        out_shape=[jax.ShapeDtypeStruct((total // 2, columns), F32)] * 2,
        scratch_shapes=[
            pltpu.VMEM((depth, 2 * columns), BF16),
            pltpu.VMEM((total, columns), F32),
        ],
        compiler_params=params(LARGE),
        cost_estimate=cost(8 * total * depth * columns, 4 * total * depth),
        name="first_coef",
    )(half, probes, a_rows, *also)


def pieces(inputs, rows):
    return [ref[i : i + rows, :] for ref in inputs for i in range(0, ref.shape[0], rows)]


def coef_kernel(rows, where, half, a_ref, *refs):
    inputs, outputs, (pair, total, sums) = refs[:-5], refs[-5:-3], refs[-3:]
    columns = inputs[0].shape[1]
    for k, value in enumerate(pieces(inputs, rows)):
        high, low = split(value)
        at = pl.ds(pl.multiple_of(where[k] * rows, rows), rows)
        pair[at, :columns] = high
        pair[at, columns:] = low
        sums[pl.ds(where[k], 1), :] = jnp.sum(value * value, axis=0, keepdims=True)
    square = jnp.sum(sums[...], axis=0, keepdims=True)
    square = jnp.sum(square, axis=1, keepdims=True)
    for out in outputs:
        out[out.shape[0] - EXTRA :, :] = jnp.broadcast_to(square, (EXTRA, out.shape[1]))
    accumulate(a_ref, pair, total, columns)
    hand_out(total, half, outputs)


def coef_terms(a_rows, basis, where, half):
    total, depth = a_rows.shape
    columns = basis[0].shape[1]
    return pl.pallas_call(
        functools.partial(coef_kernel, depth // where.shape[0]),
        in_specs=[SCALARS, SCALARS, WHOLE] + [WHOLE] * len(basis),
        out_specs=[WHOLE] * 2,
        out_shape=[jax.ShapeDtypeStruct((total // 2 + EXTRA, columns), F32)] * 2,
        scratch_shapes=[
            pltpu.VMEM((depth, 2 * columns), BF16),
            pltpu.VMEM((total, columns), F32),
            pltpu.VMEM((where.shape[0], columns), F32),
        ],
        compiler_params=params(LARGE),
        cost_estimate=cost(8 * total * depth * columns, 4 * total * depth),
        name="coef",
    )(where, half, a_rows, *basis)


def panel_kernel(sizes, squares, where, half, ranks, b_ref, mine_ref, partner_ref, *refs):
    total = refs[-1]
    clients, rows, slots = b_ref.shape
    columns = total.shape[1]
    scale = jnp.ones((1, columns), F32)
    if squares:
        square = mine_ref[mine_ref.shape[0] - EXTRA : mine_ref.shape[0] - EXTRA + 1, :]
        scale = jnp.where(square > 0, lax.rsqrt(square), 1.0)
        refs[len(sizes)][...] = jnp.broadcast_to(scale, refs[len(sizes)].shape)
    first = half[0] == 0
    for c in range(clients):
        at = pl.ds((c % (clients // 2)) * slots, slots)
        mine, partner = mine_ref[at, :], partner_ref[at, :]
        value = jnp.where(first, mine, partner) if c < clients // 2 else jnp.where(first, partner, mine)
        slot = lax.broadcasted_iota(jnp.int32, value.shape, 0)
        value = jnp.where(slot < ranks[c], value * scale, 0.0)
        term = wide_product(b_ref[c], jnp.concatenate(split(value), axis=1), columns)
        total[...] = total[...] + term if c else term
    tall = rows // sum(sizes)
    k = 0
    for out, size in zip(refs, sizes):
        for i in range(size):
            out[i * tall : (i + 1) * tall, :] = total[pl.ds(pl.multiple_of(where[k] * tall, tall), tall), :]
            k += 1


def panel_terms(b_factors, mine, partner, where, half, ranks, sizes, squares):
    clients, rows, slots = b_factors.shape
    columns = mine.shape[1]
    tall = rows // sum(sizes)
    outs = [jax.ShapeDtypeStruct((size * tall, columns), F32) for size in sizes]
    if squares:
        outs = outs + [jax.ShapeDtypeStruct((EXTRA, columns), F32)]
    return pl.pallas_call(
        functools.partial(panel_kernel, sizes, squares),
        in_specs=[SCALARS] * 3 + [WHOLE] * 3,
        out_specs=[WHOLE] * len(outs),
        out_shape=outs,
        scratch_shapes=[
            pltpu.VMEM((rows, columns), F32),
        ],
        compiler_params=params(LARGE),
        cost_estimate=cost(8 * clients * slots * rows * columns, 4 * clients * slots * rows),
        name="panel",
    )(where, half, ranks, b_factors, mine, partner)


def gram_kernel(rows, where, half, *refs):
    inputs, (other, mine), (highs, lows) = refs[:-4], refs[-4:-2], refs[-2:]
    columns = inputs[0].shape[1]
    each = len(inputs) // GROUPS
    for g in range(GROUPS):
        for k, value in enumerate(pieces(inputs[g * each : (g + 1) * each], rows)):
            high, low = split(value)
            at = pl.ds(pl.multiple_of(where[k] * rows, rows), rows)
            highs[at, g * columns : (g + 1) * columns] = high
            lows[at, g * columns : (g + 1) * columns] = low
    contract = (((0,), (0,)), ((), ()))
    high = highs[...]
    cross = lax.dot_general(high, lows[...], contract, preferred_element_type=F32)
    gram = lax.dot_general(high, high, contract, preferred_element_type=F32) + (cross + cross.T)
    tall = other.shape[0]
    first = half[0] == 0
    other[...] = jnp.where(first, gram[tall:], gram[:tall])
    mine[...] = jnp.where(first, gram[:tall], gram[tall:])


def gram_terms(panels, where, half):
    blocks = where.shape[0]
    rows, columns = panels[0][0].shape
    size = GROUPS * columns
    return pl.pallas_call(
        functools.partial(gram_kernel, rows),
        in_specs=[SCALARS, SCALARS] + [WHOLE] * sum(len(panel) for panel in panels),
        out_specs=[WHOLE] * 2,
        out_shape=[jax.ShapeDtypeStruct((size // 2, size), F32)] * 2,
        scratch_shapes=[pltpu.VMEM((blocks * rows, size), BF16)] * 2,
        compiler_params=params(LARGE),
        cost_estimate=cost(4 * blocks * rows * size * size, 4 * blocks * rows * size),
        name="gram",
    )(where, half, *[block for panel in panels for block in panel])


def iterate(gram):
    size = gram.shape[0]
    row = lax.broadcasted_iota(jnp.int32, gram.shape, 0)
    column = lax.broadcasted_iota(jnp.int32, gram.shape, 1)
    eye = jnp.where(row == column, 1.0, 0.0).astype(F32)
    trace = jnp.sum(jnp.sum(gram * eye, axis=0, keepdims=True), axis=1, keepdims=True)
    scale = lax.rsqrt(trace)
    inner = gram * scale * scale
    mixing = None
    for turn in range(NS_STEPS):
        factor = 1.5 * eye - 0.5 * inner
        high, low = split(factor)
        pair = jnp.concatenate([high, low], axis=1)
        last = turn == NS_STEPS - 1
        if turn and not last:
            both = wide_product(jnp.concatenate([inner, mixing], axis=0), pair, size)
            inner, mixing = both[:size], both[size:]
        elif turn:
            mixing = wide_product(mixing, pair, size)
        else:
            inner, mixing = wide_product(inner, pair, size), factor * scale
        if not last:
            inner = wide_product(inner, pair, size)
    return mixing


def joined(half, mine, partner):
    first = half[0] == 0
    low = jnp.where(first, mine[...], partner[...])
    high = jnp.where(first, partner[...], mine[...])
    return jnp.concatenate([low, high], axis=0)


def first_kernel(half, mine, partner, out):
    out[...] = iterate(joined(half, mine, partner))


def next_kernel(factor, half, mine, partner, before, *refs):
    scales, out = refs[:-1], refs[-1]
    columns = scales[0].shape[1]
    mixing = jnp.concatenate(
        [before[g * columns : (g + 1) * columns, :] / scales[g][0:1, 0:1] for g in range(GROUPS)], axis=0
    )
    gram = joined(half, mine, partner)
    out[...] = product(mixing, iterate(product(mixing.T, product(gram, mixing)))) * factor


def mixing_of(half, mine, partner, before=None, scales=(), factor=1.0):
    size = mine.shape[1]
    operands = (half, mine, partner) + (() if before is None else (before,) + tuple(scales))
    return pl.pallas_call(
        first_kernel if before is None else functools.partial(next_kernel, factor),
        in_specs=[SCALARS] + [WHOLE] * (len(operands) - 1),
        out_specs=WHOLE,
        out_shape=jax.ShapeDtypeStruct((size, size), F32),
        compiler_params=params(LARGE),
        cost_estimate=cost(90 * size**3, 12 * size * size),
        name="mixing",
    )(*operands)


def apply_kernel(rows, where, mixing, *refs):
    inputs, (out, held, sems) = refs[:-3], refs[-3:]
    each = len(inputs) // GROUPS
    high, low = split(mixing[...])
    copies = []
    values = [pieces(inputs[g * each : (g + 1) * each], rows) for g in range(GROUPS)]
    for k, value in enumerate(zip(*values)):
        value = jnp.concatenate(value, axis=1)
        value_high, value_low = split(value)
        held[k] = dot(value_high, high) + (dot(value_high, low) + dot(value_low, high))
        at = pl.ds(pl.multiple_of(where[k] * rows, rows), rows)
        copies.append(pltpu.make_async_copy(held.at[k], out.at[at], sems.at[k]))
        copies[k].start()
    for copy in copies:
        copy.wait()


def apply_mixing(panels, where, mixing):
    blocks = where.shape[0]
    rows, columns = panels[0][0].shape
    size = GROUPS * columns
    return pl.pallas_call(
        functools.partial(apply_kernel, rows),
        in_specs=[SCALARS] + [WHOLE] * (1 + sum(len(panel) for panel in panels)),
        out_specs=pl.BlockSpec(memory_space=pl.ANY),
        out_shape=jax.ShapeDtypeStruct((blocks * rows, size), F32),
        scratch_shapes=[pltpu.VMEM((blocks, rows, size), F32), pltpu.SemaphoreType.DMA((blocks,))],
        compiler_params=params(LARGE),
        cost_estimate=cost(6 * blocks * rows * size * size, 8 * blocks * rows * size),
        name="apply",
    )(where, mixing, *[block for panel in panels for block in panel])


class Grid:
    def __init__(self, mesh, go):
        self.go = go
        self.cohorts = mesh.shape["cohort"]
        self.feats = mesh.shape["feat"]
        self.places = self.cohorts // 2
        cohort = lax.axis_index("cohort")
        place, side = cohort // 2, cohort % 2
        self.half = (lax.axis_index("feat") % 2).astype(jnp.int32).reshape(1)
        def block(shift, side):
            return lax.rem(place + shift + self.places, self.places) * 2 + side

        ahead = self.places // 2
        self.shifts = sorted(range(ahead + 1 - self.places, ahead + 1), key=lambda d: (abs(d), -d))
        outward, inward = self.shifts[::-1], [-d for d in self.shifts]
        self.scatter_order = jnp.stack([block(d, s) for s in (1 - side, side) for d in outward]).astype(jnp.int32)
        self.gather_order = jnp.stack([block(d, s) for s in (side, 1 - side) for d in inward]).astype(jnp.int32)
        places = range(self.places)
        cuts = [0] + list(places)[FIRST_OUT :: NEXT_OUT] + [self.places]
        self.outs = [b - a for a, b in zip(cuts, cuts[1:])]
        self.sizes = self.outs + [1] * self.places
        cuts = [0] + list(places)[1::NEXT_IN] + [self.places]
        self.ins = list(zip(cuts, cuts[1:]))

    def across(self, block):
        return lax.ppermute(block, "cohort", [(i, i ^ 1) for i in range(self.cohorts)])

    def along(self, block, way):
        step = 2 if way > 0 else self.cohorts - 2
        return lax.ppermute(block, "cohort", [(i, (i + step) % self.cohorts) for i in range(self.cohorts)])

    def feat_swap(self, block, bit):
        return lax.ppermute(block, "feat", [(i, i ^ bit) for i in range(self.feats)])

    def feat_sum(self, other, mine, after=None, before_last=None):
        total = mine + self.feat_swap(other, 1)
        if after is not None:
            total = self.follow(total, after)
        bit = 2
        while bit < self.feats:
            total = total + self.feat_swap(total, bit)
            bit *= 2
        return total, self.feat_swap(total if before_last is None else self.follow(total, before_last), 1)

    def follow(self, block, earlier):
        rows, columns = (min(a, b) for a, b in zip(block.shape, earlier.shape))
        if rows < block.shape[0]:
            return jnp.concatenate([jnp.where(self.go, block[:rows], earlier[:rows, :columns]), block[rows:]], 0)
        return jnp.where(self.go, block, earlier[:rows, :columns])

    def scatter_sum(self, terms, early=None, turn=None):
        keep = terms[len(self.outs) :]
        rows = keep[0].shape[0]
        carried, step = {}, 0
        for i, size in enumerate(self.outs):
            send = terms[i]
            if i and early is not None:
                send = self.follow(send, early)
            if not i and turn is not None:
                send = self.follow(send, turn)
            arrived = self.across(send)
            if not i:
                arrival = arrived
            for j in range(size):
                shift = self.shifts[self.places - 1 - step]
                total = arrived[j * rows : (j + 1) * rows] + keep[step]
                step += 1
                way = (shift > 0) - (shift < 0)
                for carry in [carried.get(way)] if way else carried.values():
                    total = total if carry is None else total + carry
                if way:
                    carried[way] = self.along(total, way)
        return total, arrival

    def gather(self, block, early=None):
        carried = {0: block, 1: block, -1: block}
        near, far = [], []
        for first, end in self.ins:
            group = []
            for step in range(first, end):
                way = (self.shifts[step] > 0) - (self.shifts[step] < 0)
                if way:
                    if HOLD and step >= 3:
                        carried[way] = self.follow(carried[way], far[(step - 3) // NEXT_IN])
                    carried[way] = self.along(carried[way], way)
                group.append(carried[way])
            group = jnp.concatenate(group, 0) if len(group) > 1 else group[0]
            near.append(group)
            if early is not None and end == self.places:
                group = self.follow(group, early)
            far.append(self.across(group))
        return near + far


def solution(mesh):
    def on_device(b_factors, a_factors, ranks, probes):
        grid = Grid(mesh, ranks[0] > 0)
        clients, rows, slots = b_factors.shape
        a_rows = a_factors.reshape(clients * slots, rows)

        def mixing_after(mixing, panels, scales, factor):
            gram = grid.feat_sum(*gram_terms(panels, grid.gather_order, grid.half))
            return mixing_of(grid.half, *gram, mixing, scales if mixing is not None else (), factor)

        mixing, panels = None, None
        for turn in range(ITERS):
            squares = turn > 0
            if turn == 0:
                halves = [first_coef(a_rows, probes, g, grid.half, [b_factors] if g else []) for g in range(GROUPS)]
            else:
                halves = [coef_terms(a_rows, panel, grid.gather_order, grid.half) for panel in panels]
            terms, mine = [], None
            for g in range(GROUPS):
                before_last = terms[-1][0] if g and SWAP_GATE else None
                mine, partner = grid.feat_sum(*halves[g], mine, before_last)
                terms.append(
                    panel_terms(b_factors, mine, partner, grid.scatter_order, grid.half, ranks, grid.sizes, squares)
                )
            scales = [array for term in terms for array in term[len(grid.sizes) :]]
            terms = [term[: len(grid.sizes)] for term in terms]
            totals, arrival = [], None
            for g, term in enumerate(terms):
                early = terms[-1][-1] if g < GROUPS - 1 and PANELS_FIRST else None
                total, arrival = grid.scatter_sum(term, early, arrival if IN_TURN else None)
                totals.append(total)
            if turn:
                first = panels[0]
                if LATE_GRAM:
                    first = [grid.follow(first[0], totals[0])] + first[1:]
                mixing = mixing_after(mixing, [first] + panels[1:], before_scales, 1.0)
            panels = [grid.gather(total, mixing if g else None) for g, total in enumerate(totals)]
            before_scales = scales
        mixing = mixing_after(mixing, panels, scales, math.sqrt(rows * grid.feats))
        return apply_mixing(panels, grid.gather_order, mixing)

    in_specs = (P("cohort", "feat", None), P("cohort", None, "feat"), P("cohort"), P("feat", None))
    return jax.shard_map(on_device, mesh=mesh, in_specs=in_specs, out_specs=P("feat", None), check_vma=False)
```
